32 devices in a mesh: dp: 8 (over y, x, core), ctx: 4 (over z).
Axes of the slice: x: 2, y: 2, z: 4, core: 2. Of those that a mesh axis runs over, the one named last changes fastest.
Arguments:
- queries: bfloat16 [4096, 32, 128], P(('ctx', 'dp')), may hold values from -8 to 8
- keys: bfloat16 [4096, 8, 128], P(('ctx', 'dp')), may hold values from -8 to 8
- values: bfloat16 [4096, 8, 128], P(('ctx', 'dp')), may hold values from -6 to 6
- doc_blocks: int32 [16], replicated, may hold values from 1 to 4, 32 in all
Outputs:
- attended: bfloat16 [4096, 32, 128], P(('ctx', 'dp'))
The draws below stay inside these ranges and needn't reach their ends.
Inputs may be any that keep to these rules, and one draw needn't show every extreme that they name: `doc_blocks`: lengths in blocks of 128 tokens; they sum to 32 and the longest is exactly 4.
All inputs are finite; a program needn't handle non-finite values.
Results may differ from the reference program's by a relative error of at most 0.0037.
Values may be sent and summed in bfloat16 or wider, within the bound.
No kernel may reach another device: no remote copies, remote signals or barrier semaphores. Data moves between devices by JAX's collectives and lax.ppermute only.
A program may use at most 128 MiB of HBM per device.

```python
import math
import jax
import jax.numpy as jnp
import numpy as np
from jax import lax

QH = 32
KVH = 8
HD = 128
BLK = 128
TOK_DEV = 128
TOKENS = 4096
NBLK = 32
MAXDOC_BLK = 4
NDOCS = 16
N_DP = 8
N_CTX = 4


def draw_queries(key, part):
    key = jax.random.fold_in(key, 1)
    entries = jnp.clip(jax.random.normal(key, (TOKENS, QH, HD), jnp.float32), -6.0, 6.0)
    return entries.astype(jnp.bfloat16)


def draw_keys(key, part):
    key = jax.random.fold_in(key, 2)
    entries = jnp.clip(jax.random.normal(key, (TOKENS, KVH, HD), jnp.float32), -6.0, 6.0)
    return entries.astype(jnp.bfloat16)


def shard_levels(own_key, dims, split, smallest, top_value):
    factor_of, own = 1.0, jax.random.fold_in(own_key, 6)
    for dim, parts in split:
        heights = jnp.exp(jax.random.uniform(jax.random.fold_in(own, dim), (parts,), jnp.float32, smallest / len(split), top_value / len(split)))
        factor_of = factor_of * jnp.repeat(heights, dims[dim] // parts).reshape([-1 if axis == dim else 1 for axis in range(len(dims))])
    return factor_of


def length_profile(count, total, most, skew):
    portions = [(1 << 20) // math.isqrt(standing ** skew) + 1 for standing in range(2, count + 1)]
    spare, holding = total - most - (count - 1), [1] * (count - 1)
    while spare > 0:
        candidates = [i for i in range(count - 1) if holding[i] < most]
        pool, left = sum([portions[i] for i in candidates]), spare
        for i in candidates:
            more = min(most - holding[i], max(1, left * portions[i] // pool), spare)
            holding[i] = holding[i] + more
            spare = spare - more
    return np.array([most] + holding)


def ragged_sizes(key, number_of, total, limit, slope):
    if number_of == 2:
        one = jax.random.randint(key, (), max(1, total - limit), min(limit, total - 1) + 1)
        return jnp.stack([one, total - one])
    tallies = jnp.asarray(length_profile(number_of, total, limit, slope), jnp.int32)
    pairs = (number_of - 1) // 2
    source_of, taker = tallies[1:1 + 2 * pairs:2], tallies[2:2 + 2 * pairs:2]
    slack = jnp.minimum(source_of - 1, limit - taker)
    moved = jax.random.randint(jax.random.fold_in(key, 1), (pairs,), 0, 1 << 20) % (slack + 1)
    tallies = tallies.at[1:1 + 2 * pairs:2].set(source_of - moved).at[2:2 + 2 * pairs:2].set(taker + moved)
    return tallies[jax.random.permutation(jax.random.fold_in(key, 2), number_of)]


def bell_draw(stream_key, shape, scale, limit, pieces=(), kind=jnp.bfloat16):
    factor_of = shard_levels(stream_key, shape, pieces, -0.22, 0.18) if pieces else 1.0
    result = jax.random.normal(stream_key, shape, jnp.float32) * scale * factor_of
    return jnp.minimum(jnp.maximum(result, -limit), limit).astype(kind)


def setup_inputs(seed: int = 0) -> dict:
    key_of = jax.random.split(jax.random.key(seed), 5)
    queries = draw_queries(jax.random.fold_in(key_of[4], 71), 0)
    keys = draw_keys(jax.random.fold_in(key_of[4], 71), 0)
    values = bell_draw(key_of[2], (TOKENS, KVH, HD), 1.0, 6.0, ((0, 32),))
    doc_blocks = ragged_sizes(key_of[3], NDOCS, NBLK, MAXDOC_BLK, 2).astype(jnp.int32)
    return dict(queries=queries, keys=keys, values=values, doc_blocks=doc_blocks)


def token_docs(doc_blocks, first_block, count, block):
    doc_ends = jnp.cumsum(doc_blocks, dtype=jnp.int32)
    blocks = first_block + jnp.arange(count, dtype=jnp.int32)
    owners = jnp.sum((doc_ends[None, :] <= blocks[:, None]).astype(jnp.int32), axis=1, dtype=jnp.int32)
    owners = jnp.where(blocks < 0, -1, owners)
    return jnp.repeat(owners, block)


def reference(queries, keys, values, doc_blocks):
    key_span = MAXDOC_BLK * BLK
    tile_rows = TOK_DEV * N_DP // N_CTX
    width = key_span + tile_rows
    group_size = QH // KVH
    key_docs = token_docs(doc_blocks, -MAXDOC_BLK, MAXDOC_BLK + NBLK, BLK)
    zero_rows = jnp.zeros((key_span, KVH, HD), jnp.bfloat16)
    key_buffer = jnp.concatenate([zero_rows, keys], axis=0)
    value_buffer = jnp.concatenate([zero_rows, values], axis=0)
    causal = jnp.arange(width)[None, :] <= key_span + jnp.arange(tile_rows)[:, None]
    score_scale = HD ** -0.5

    def one_tile(tile_index):
        offset = tile_index * tile_rows
        key_window = lax.dynamic_slice_in_dim(key_buffer, offset, width, 0)
        value_window = lax.dynamic_slice_in_dim(value_buffer, offset, width, 0)
        window_docs = lax.dynamic_slice_in_dim(key_docs, offset, width, 0)
        query_docs = lax.dynamic_slice_in_dim(key_docs, offset + key_span, tile_rows, 0)
        query_tile = lax.dynamic_slice_in_dim(queries, offset, tile_rows, 0)
        query_tile = query_tile.reshape(tile_rows, KVH, group_size, HD)
        allowed = (window_docs[None, :] == query_docs[:, None]) & causal
        scores = jnp.einsum("qgrd,kgd->grqk", query_tile.astype(jnp.float32), key_window.astype(jnp.float32)) * score_scale
        scores = jnp.where(allowed[None, None], scores, -jnp.inf)
        row_max = jnp.max(scores, axis=3, keepdims=True)
        weights = jnp.exp(scores - row_max)
        totals = jnp.sum(weights, axis=3)
        rounded = lax.optimization_barrier(weights.astype(jnp.bfloat16)).astype(jnp.float32)
        combined = jnp.einsum("grqk,kgd->qgrd", rounded, value_window.astype(jnp.float32))
        return (combined / jnp.transpose(totals, (2, 0, 1))[..., None]).astype(jnp.bfloat16)

    tiles = lax.map(one_tile, jnp.arange(TOKENS // tile_rows, dtype=jnp.int32))
    return tiles.reshape(TOKENS, QH, HD)
```

```python
import functools

import jax
import jax.numpy as jnp
from jax import lax
from jax.experimental import pallas as pl
from jax.experimental.pallas import tpu as pltpu
from jax.sharding import PartitionSpec as P

LOG2E = 1.4426950408889634
MIB = 1 << 20
VMEM = pl.BlockSpec(memory_space=pltpu.VMEM)
SMEM = pl.BlockSpec(memory_space=pltpu.SMEM)
ANY = pl.BlockSpec(memory_space=pl.ANY)
HBM = pl.BlockSpec(memory_space=pltpu.HBM)
LANES = 128
GROUP = 4
EIGHT = 2 * GROUP
TILE = 64


def pack_kernel(k_ref, v_ref, out_ref, longer_ref, keys_ref, values_ref, near, wide, sems):
    _, rows, heads, size = near.shape
    copies = [pltpu.make_async_copy(ref, near.at[n], sems.at[n]) for n, ref in enumerate((k_ref, v_ref))]
    for copy in copies:
        copy.start()
    for n, copy in enumerate(copies):
        copy.wait()
        wide[n] = near[n].astype(jnp.float32).reshape(rows * heads, size)
        for g in range(heads):
            part = wide[n, pl.ds(g, rows, stride=heads), :].astype(jnp.bfloat16)
            part = part.T if n == 0 else part
            lanes = slice(g * size, (g + 1) * size)
            for ref in (out_ref, longer_ref):
                ref[n * rows : (n + 1) * rows, lanes] = part
            (keys_ref, values_ref)[n][:, lanes] = part


def pack(keys, values):
    rows, heads, size = keys.shape
    assert rows == size
    keys, values = (pltpu.with_memory_space_constraint(x, pltpu.HBM) for x in (keys, values))
    heights = 2 * rows, 2 * rows + 8, rows, rows
    return pl.pallas_call(
        pack_kernel,
        out_shape=tuple(jax.ShapeDtypeStruct((height, heads * size), jnp.bfloat16) for height in heights),
        in_specs=[HBM, HBM],
        out_specs=(VMEM,) * len(heights),
        scratch_shapes=[
            pltpu.VMEM((2, rows, heads, size), jnp.bfloat16),
            pltpu.VMEM((2, rows * heads, size), jnp.float32),
            pltpu.SemaphoreType.DMA((2,)),
        ],
        compiler_params=pltpu.CompilerParams(vmem_limit_bytes=8 * MIB),
        name="pack_kv",
    )(keys, values)


def blocks_before(doc_ref, block):
    def step(j, carry):
        end, start = carry
        end = end + doc_ref[j]
        return end, jnp.where(end <= block, end, start)

    _, start = lax.fori_loop(0, doc_ref.shape[0], step, (jnp.int32(0), jnp.int32(0)))
    return block - start


def low_rows(rows, lanes):
    return lax.broadcasted_iota(jnp.int32, (rows, lanes), 0) % EIGHT < GROUP


def keys_of(blocks, j, rows):
    at = 2 * j * rows
    pairs = [jnp.concatenate([ref[:rows, at : at + rows], ref[:rows, at + rows : at + 2 * rows]], axis=0) for ref, _ in blocks]
    return jnp.concatenate(pairs, axis=1)


def values_of(blocks, j, rows):
    lanes = slice(2 * j * rows, 2 * (j + 1) * rows)
    tops = [rows if ref.shape[0] > rows else 0 for _, ref in blocks]
    return jnp.concatenate([ref[top : top + rows, lanes] for top, (_, ref) in zip(tops, blocks)], axis=0)


def dot(a, b):
    return jnp.dot(a, b, preferred_element_type=jnp.float32)


def prepare_kernel(doc_ref, q_ref, lhs_ref, before_ref, lengths, near, sems):
    rows, heads, size = near.shape
    tall = TILE * EIGHT
    low = low_rows(tall, size)
    spans = [pl.ds(t * TILE, TILE) for t in range(rows // TILE)]
    copies = [pltpu.make_async_copy(doc_ref, lengths, sems.at[len(spans)])]
    copies += [pltpu.make_async_copy(q_ref.at[span], near.at[span], sems.at[t]) for t, span in enumerate(spans)]
    for copy in copies:
        copy.start()
    copies[0].wait()
    block = lax.axis_index("ctx") * lax.axis_size("dp") + lax.axis_index("dp")
    before_ref[...] = jnp.full(before_ref.shape, blocks_before(lengths, block), jnp.int32)
    for t, span in enumerate(spans):
        copies[1 + t].wait()
        for j in range(heads // EIGHT):
            if j % 2 == 0:
                q16 = near[span, j * EIGHT : (j + 2) * EIGHT, :].astype(jnp.float32)
            q8 = q16[:, j % 2 * EIGHT : (j % 2 + 1) * EIGHT, :].reshape(tall, size)
            lhs = jnp.concatenate([jnp.where(low, q8, 0.0), jnp.where(low, 0.0, q8)], axis=1)
            lhs_ref[j, t * tall : (t + 1) * tall, :] = lhs.astype(jnp.bfloat16)


def prepare(doc_blocks, queries):
    rows, heads, size = queries.shape
    doc_blocks, queries = (pltpu.with_memory_space_constraint(x, pltpu.HBM) for x in (doc_blocks, queries))
    return pl.pallas_call(
        prepare_kernel,
        out_shape=(
            jax.ShapeDtypeStruct((heads // EIGHT, rows * EIGHT, 2 * size), jnp.bfloat16),
            jax.ShapeDtypeStruct((EIGHT, LANES), jnp.int32),
        ),
        in_specs=[HBM, HBM],
        out_specs=(VMEM, VMEM),
        scratch_shapes=[
            pltpu.SMEM(doc_blocks.shape, jnp.int32),
            pltpu.VMEM(queries.shape, jnp.bfloat16),
            pltpu.SemaphoreType.DMA((rows // TILE + 1,)),
        ],
        compiler_params=pltpu.CompilerParams(vmem_limit_bytes=12 * MIB),
        cost_estimate=pl.CostEstimate(flops=1024, bytes_accessed=1024, transcendentals=0),
        name="prepare",
    )(doc_blocks, queries)


def attend_kernel(cases, scale, merges, keeps, gives, blocks_of, *refs):
    refs = list(refs)
    lhs_ref, before_ref = refs[:2]
    del refs[:2]
    if merges:
        state_ref = refs[:3]
        del refs[:3]
    count = max(at for block in blocks_of for at in block) + 1
    given = [(refs[a], refs[b]) for a, b in blocks_of]
    del refs[:count]
    if gives == "given":
        del refs[0]
    if keeps:
        state_out = refs[:3]
        del refs[:3]
    if gives:
        out_ref, held, sems = refs
    js, size = lhs_ref.shape[0], lhs_ref.shape[2] // 2
    rows = lhs_ref.shape[1] // EIGHT
    place = lax.axis_index("dp")
    before = jnp.max(before_ref[...])

    def out_copy(t, tokens):
        return pltpu.make_async_copy(held.at[tokens], out_ref.at[tokens], sems.at[t])

    def add(blocks, last):
        tall = TILE * EIGHT
        low = low_rows(tall, size)
        if not merges:
            token = lax.broadcasted_iota(jnp.int32, (tall, rows), 0) // EIGHT
            spot = lax.broadcasted_iota(jnp.int32, (tall, rows), 1)
        for t in range(rows // TILE):
            tokens, here, outs = pl.ds(t * TILE, TILE), pl.ds(t * tall, tall), []
            for j in range(js):
                if merges:
                    old, total, mixed = (ref[j, here, :] for ref in state_ref)
                if blocks:
                    s = dot(lhs_ref[j, here, :], keys_of(blocks, j, rows))
                    s = [s[:, n * rows : (n + 1) * rows] for n in range(len(blocks))]
                    if not merges:
                        s[0] = jnp.where(spot <= token + t * TILE, s[0], -jnp.inf)
                    top = jnp.max(functools.reduce(jnp.maximum, s), axis=1, keepdims=True)
                    if merges:
                        top = jnp.maximum(old, top)
                        keep = jnp.exp2((old - top) * scale)
                    w = [jnp.exp2((part - top) * scale) for part in s]
                    found = dot(jnp.concatenate(w, axis=1).astype(jnp.bfloat16), values_of(blocks, j, rows))
                    found = jnp.where(low, found[:, :size], found[:, size:])
                    fresh = functools.reduce(jnp.add, w)
                    mixed = found + keep * mixed if merges else found
                    total = fresh + keep * total if merges else fresh
                if last:
                    total = jnp.sum(total, axis=1, keepdims=True)
                    guess = pl.reciprocal(total, approx=True)
                    guess = guess * (2.0 - total * guess)
                    outs.append((mixed * guess).reshape(TILE, EIGHT, size))
                    if j % 2:
                        held[tokens, (j - 1) * EIGHT : (j + 1) * EIGHT, :] = jnp.concatenate(
                            outs[-2:], axis=1
                        ).astype(jnp.bfloat16)
                else:
                    state_out[0][j, here, :] = jnp.broadcast_to(top, (tall, LANES))
                    state_out[1][j, here, :] = total
                    state_out[2][j, here, :] = mixed
            if last:
                out_copy(t, tokens).start()
        if last:
            for t in range(rows // TILE):
                out_copy(t, pl.ds(t * TILE, TILE)).wait()

    for wheres, chosen, last in cases:
        fits = False
        for parity, least, end in wheres:
            fit = before >= least
            if end is not None:
                fit = jnp.logical_and(fit, before < end)
            if parity is not None:
                fit = jnp.logical_and(fit, place % 2 == parity)
            fits = fit if fits is False else jnp.logical_or(fits, fit)
        pl.when(fits)(functools.partial(add, [given[at] for at in chosen], last))


def attend(name, shape, prepared, kvs, cases, state=(), keeps=False, gives="", given=None, in_place=False):
    rows, heads, size = shape
    js, tall = heads // EIGHT, rows * EIGHT
    arrays, blocks_of = [], []
    for block in kvs:
        block = block if isinstance(block, tuple) else (block,)
        blocks_of.append((len(arrays), len(arrays) + len(block) - 1))
        arrays += block
    inputs = [*prepared, *state, *arrays]
    specs = [VMEM] * len(inputs)
    outs = [jax.ShapeDtypeStruct((js, tall, LANES), jnp.float32)] * (3 if keeps else 0)
    out_specs = [VMEM] * len(outs)
    aliases = {2: 0, 3: 1, 4: 2} if in_place else {}
    if gives == "given":
        aliases[len(inputs)] = len(outs)
        inputs.append(given)
        specs.append(ANY)
    if gives:
        outs.append(jax.ShapeDtypeStruct(shape, jnp.bfloat16))
        out_specs.append(ANY)
    scale = LOG2E * size ** (-0.5)
    return pl.pallas_call(
        functools.partial(attend_kernel, cases, scale, bool(state), keeps, gives, blocks_of),
        out_shape=tuple(outs),
        in_specs=specs,
        out_specs=tuple(out_specs),
        input_output_aliases=aliases,
        scratch_shapes=[pltpu.VMEM(shape, jnp.bfloat16), pltpu.SemaphoreType.DMA((rows // TILE,))] if gives else [],
        compiler_params=pltpu.CompilerParams(vmem_limit_bytes=24 * MIB),
        cost_estimate=pl.CostEstimate(flops=1024, bytes_accessed=1024, transcendentals=0),
        name=name,
    )(*inputs)


def on_device(axes, dp, ctx, queries, keys, values, doc_blocks):
    own, longer, own_keys, own_values = pack(keys, values)
    count, farthest = dp * ctx, dp // 2 - 1
    def moved(array, target_of):
        def at(block):
            return block % dp * ctx + block // dp if axes[0] == "dp" else block

        route = [(i, target_of(i)) for i in range(count)]
        return lax.ppermute(array, axes, [(at(i), at(to)) for i, to in route if to is not None and to < count])

    if farthest == 3:
        crossed = moved(own, lambda i: i + 1 if i % 2 else i + 3)
        beside = tuple(moved(part, lambda i: None if i % 2 else i + 1) for part in (own_keys, own_values))
        queries, beside = lax.optimization_barrier((queries, beside))
        prepared = prepare(doc_blocks, queries)
        call = functools.partial(attend, shape=queries.shape, prepared=prepared)
        *state, out = call(
            "own_blocks",
            kvs=[own, beside],
            cases=[
                ([(None, 0, 1)], [0], True),
                ([(1, 1, 2)], [0, 1], True),
                ([(0, 1, None)], [0], False),
                ([(1, 2, None)], [0, 1], False),
            ],
            keeps=True,
            gives="fresh",
        )
        longer, out = lax.optimization_barrier((longer, out))
        behind = moved(longer, lambda i: i + 3 if i % 2 else None)
        crossed, out = lax.optimization_barrier((crossed, out))
        swapped = moved(crossed, lambda i: i ^ 1)
        (out,) = call("nearest", kvs=[own, crossed], cases=[([(0, 1, 2)], [0, 1], True)], gives="given", given=out)
        *state, out = call(
            "swapped_blocks",
            kvs=[crossed, swapped],
            cases=[
                ([(0, 2, 3), (1, 3, None)], [0, 1], True),
                ([(0, 3, None)], [0, 1], False),
                ([(1, 2, 3)], [1], True),
            ],
            state=state,
            keeps=True,
            gives="given",
            given=out,
        )
        (out,) = call(
            "farthest", kvs=[behind], cases=[([(0, 3, None)], [0], True)], state=state, gives="given", given=out
        )
        return out
    call = functools.partial(attend, shape=queries.shape, prepared=prepare(doc_blocks, queries))
    state = call("own_blocks", kvs=[own], cases=[([(None, 0, None)], [0], False)], keeps=True)
    shifted = [moved(own, lambda i, m=m: i + 2 * m) for m in range(1, (farthest - 1) // 2 + 1)]
    alone = moved(longer, lambda i: i + farthest if i % 2 else i + 1)
    shifted, state = lax.optimization_barrier((shifted, state))
    for m, block in enumerate(shifted, 1):
        other = moved(block, lambda i: i ^ 1)
        cases = [
            ([(0, 2 * m - 1, 2 * m)], [1], False),
            ([(0, 2 * m, None), (1, 2 * m + 1, None)], [0, 1], False),
            ([(1, 2 * m, 2 * m + 1)], [0], False),
        ]
        state = call("more_blocks", kvs=[block, other], cases=cases, state=state, keeps=True, in_place=True)
    cases = [
        ([(0, farthest, None), (1, 1, None)], [0], True),
        ([(0, 0, farthest), (1, 0, 1)], [], True),
    ]
    (out,) = call("farthest", kvs=[alone], cases=cases, state=state, gives="fresh")
    return out


def solution(mesh):
    dp, ctx = mesh.shape["dp"], mesh.shape["ctx"]
    placed = P(("ctx", "dp"), None, None)
    return jax.shard_map(
        functools.partial(on_device, tuple(mesh.axis_names), dp, ctx),
        mesh=mesh,
        in_specs=(placed, placed, placed, P()),
        out_specs=placed,
        check_vma=False,
    )
```

```python
import functools

import jax
import jax.numpy as jnp
from jax import lax
from jax.experimental import pallas as pl
from jax.experimental.pallas import tpu as pltpu
from jax.sharding import PartitionSpec as P

LOG2E = 1.4426950408889634
MIB = 1 << 20
VMEM = pl.BlockSpec(memory_space=pltpu.VMEM)
SMEM = pl.BlockSpec(memory_space=pltpu.SMEM)
ANY = pl.BlockSpec(memory_space=pl.ANY)
HBM = pl.BlockSpec(memory_space=pltpu.HBM)
LANES = 128
GROUP = 4
EIGHT = 2 * GROUP
LARGE, SMALL = 64, 32


def lay_out(refs, wide, write):
    for n, ref in enumerate(refs):
        rows, heads, size = ref.shape
        wide[n] = ref[...].astype(jnp.float32).reshape(rows * heads, size)
        for g in range(heads):
            part = wide[n, pl.ds(g, rows, stride=heads), :].astype(jnp.bfloat16)
            write(slice(n * rows, (n + 1) * rows), slice(g * size, (g + 1) * size), part.T if n == 0 else part)


def pack_kernel(k_ref, v_ref, out_ref, wide):
    def write(rows, lanes, part):
        out_ref[rows, lanes] = part

    lay_out((k_ref, v_ref), wide, write)


def pack(keys, values):
    rows, heads, size = keys.shape
    return pl.pallas_call(
        pack_kernel,
        out_shape=jax.ShapeDtypeStruct((2 * rows, heads * size), jnp.bfloat16),
        in_specs=[VMEM, VMEM],
        out_specs=VMEM,
        scratch_shapes=[pltpu.VMEM((2, rows * heads, size), jnp.float32)],
        compiler_params=pltpu.CompilerParams(vmem_limit_bytes=8 * MIB),
        cost_estimate=pl.CostEstimate(flops=1024, bytes_accessed=1024, transcendentals=0),
        name="pack_kv",
    )(keys, values)


def blocks_before(doc_ref, block):
    def step(j, carry):
        end, start = carry
        end = end + doc_ref[j]
        return end, jnp.where(end <= block, end, start)

    _, start = lax.fori_loop(0, doc_ref.shape[0], step, (jnp.int32(0), jnp.int32(0)))
    return block - start


def low_rows(rows, lanes):
    return lax.broadcasted_iota(jnp.int32, (rows, lanes), 0) % EIGHT < GROUP


def keys_of(blocks, j, rows):
    at = 2 * j * rows
    pairs = [jnp.concatenate([ref[:rows, at : at + rows], ref[:rows, at + rows : at + 2 * rows]], axis=0) for ref, _ in blocks]
    return jnp.concatenate(pairs, axis=1)


def values_of(blocks, j, rows):
    lanes = slice(2 * j * rows, 2 * (j + 1) * rows)
    tops = [rows if ref.shape[0] > rows else 0 for _, ref in blocks]
    return jnp.concatenate([ref[top : top + rows, lanes] for top, (_, ref) in zip(tops, blocks)], axis=0)


def dot(a, b):
    return jnp.dot(a, b, preferred_element_type=jnp.float32)


def prepare_kernel(doc_ref, q_ref, k_ref, v_ref, lhs_ref, before_ref, *refs):
    *out_refs, lengths, near_q, near_k, near_v, wide, sems = refs
    rows, heads, size = near_q.shape
    tall = SMALL * EIGHT
    low = low_rows(tall, size)
    spans = [pl.ds(t * SMALL, SMALL) for t in range(rows // SMALL)]
    pairs = [(k_ref, near_k), (v_ref, near_v), (doc_ref, lengths)]
    pairs += [(q_ref.at[span], near_q.at[span]) for span in spans]
    copies = [pltpu.make_async_copy(*pair, sems.at[n]) for n, pair in enumerate(pairs)]
    for copy in copies:
        copy.start()
    for copy in copies[:3]:
        copy.wait()

    def write(rows, lanes, part):
        for ref in out_refs:
            ref[rows, lanes] = part

    lay_out((near_k, near_v), wide, write)
    block = lax.axis_index("ctx") * lax.axis_size("dp") + lax.axis_index("dp")
    before_ref[...] = jnp.full(before_ref.shape, blocks_before(lengths, block), jnp.int32)
    for t, span in enumerate(spans):
        copies[3 + t].wait()
        for j in range(heads // EIGHT):
            if j % 2 == 0:
                q16 = near_q[span, j * EIGHT : (j + 2) * EIGHT, :].astype(jnp.float32)
            q8 = q16[:, j % 2 * EIGHT : (j % 2 + 1) * EIGHT, :].reshape(tall, size)
            lhs = jnp.concatenate([jnp.where(low, q8, 0.0), jnp.where(low, 0.0, q8)], axis=1)
            lhs_ref[j, t * tall : (t + 1) * tall, :] = lhs.astype(jnp.bfloat16)


def prepare(doc_blocks, queries, keys, values, pads):
    rows, heads, size = queries.shape
    kv_heads = keys.shape[1]
    arrays = [pltpu.with_memory_space_constraint(x, pltpu.HBM) for x in (doc_blocks, queries, keys, values)]
    return pl.pallas_call(
        prepare_kernel,
        out_shape=(
            jax.ShapeDtypeStruct((heads // EIGHT, rows * EIGHT, 2 * size), jnp.bfloat16),
            jax.ShapeDtypeStruct((EIGHT, LANES), jnp.int32),
            *(jax.ShapeDtypeStruct((2 * rows + pad, kv_heads * size), jnp.bfloat16) for pad in pads),
        ),
        in_specs=[HBM] * 4,
        out_specs=(VMEM,) * (2 + len(pads)),
        scratch_shapes=[
            pltpu.SMEM(doc_blocks.shape, jnp.int32),
            pltpu.VMEM(queries.shape, jnp.bfloat16),
            pltpu.VMEM(keys.shape, jnp.bfloat16),
            pltpu.VMEM(values.shape, jnp.bfloat16),
            pltpu.VMEM((2, rows * kv_heads, size), jnp.float32),
            pltpu.SemaphoreType.DMA((rows // SMALL + 3,)),
        ],
        compiler_params=pltpu.CompilerParams(vmem_limit_bytes=16 * MIB),
        cost_estimate=pl.CostEstimate(flops=1024, bytes_accessed=1024, transcendentals=0),
        name="prepare",
    )(*arrays)


def attend_kernel(cases, scale, merges, keeps, gives, blocks_of, *refs):
    refs = list(refs)
    lhs_ref, before_ref = refs[:2]
    del refs[:2]
    if merges:
        state_ref = refs[:3]
        del refs[:3]
    count = max(at for block in blocks_of for at in block) + 1
    given = [(refs[a], refs[b]) for a, b in blocks_of]
    del refs[:count]
    if gives == "given":
        del refs[0]
    if keeps:
        state_out = refs[:3]
        del refs[:3]
    if gives:
        out_ref, held, sems = refs
    js, size = lhs_ref.shape[0], lhs_ref.shape[2] // 2
    rows = lhs_ref.shape[1] // EIGHT
    place = lax.axis_index("dp")
    before = jnp.max(before_ref[...])

    def out_copy(t, pair, tile):
        part = pl.ds(t * tile, tile), pl.ds(pair * 2 * EIGHT, 2 * EIGHT)
        return pltpu.make_async_copy(held.at[part], out_ref.at[part], sems.at[t, pair])

    def add(blocks, last):
        tile = SMALL if len(blocks) < 2 else LARGE
        tall = tile * EIGHT
        low = low_rows(tall, size)
        if not merges:
            token = lax.broadcasted_iota(jnp.int32, (tall, rows), 0) // EIGHT
            spot = lax.broadcasted_iota(jnp.int32, (tall, rows), 1)
        for t in range(rows // tile):
            tokens, here, outs = pl.ds(t * tile, tile), pl.ds(t * tall, tall), []
            for j in range(js):
                if merges:
                    old, total, mixed = (ref[j, here, :] for ref in state_ref)
                if blocks:
                    s = dot(lhs_ref[j, here, :], keys_of(blocks, j, rows))
                    s = [s[:, n * rows : (n + 1) * rows] for n in range(len(blocks))]
                    if not merges:
                        s[0] = jnp.where(spot <= token + t * tile, s[0], -jnp.inf)
                    top = jnp.max(functools.reduce(jnp.maximum, s), axis=1, keepdims=True)
                    if merges:
                        top = jnp.maximum(old, top)
                        keep = jnp.exp2((old - top) * scale)
                    w = [jnp.exp2((part - top) * scale) for part in s]
                    found = dot(jnp.concatenate(w, axis=1).astype(jnp.bfloat16), values_of(blocks, j, rows))
                    found = jnp.where(low, found[:, :size], found[:, size:])
                    fresh = functools.reduce(jnp.add, w)
                    mixed = found + keep * mixed if merges else found
                    total = fresh + keep * total if merges else fresh
                if last:
                    total = jnp.sum(total, axis=1, keepdims=True)
                    outs.append((mixed * pl.reciprocal(total, approx=True)).reshape(tile, EIGHT, size))
                    if j % 2:
                        held[tokens, (j - 1) * EIGHT : (j + 1) * EIGHT, :] = jnp.concatenate(
                            outs[-2:], axis=1
                        ).astype(jnp.bfloat16)
                        out_copy(t, j // 2, tile).start()
                else:
                    state_out[0][j, here, :] = jnp.broadcast_to(top, (tall, LANES))
                    state_out[1][j, here, :] = total
                    state_out[2][j, here, :] = mixed
        if last:
            for t in range(rows // tile):
                for pair in range(js // 2):
                    out_copy(t, pair, tile).wait()

    for wheres, chosen, last in cases:
        fits = False
        for parity, least, end in wheres:
            fit = before >= least
            if end is not None:
                fit = jnp.logical_and(fit, before < end)
            if parity is not None:
                fit = jnp.logical_and(fit, place % 2 == parity)
            fits = fit if fits is False else jnp.logical_or(fits, fit)
        pl.when(fits)(functools.partial(add, [given[at] for at in chosen], last))


def attend(name, shape, prepared, kvs, cases, state=(), keeps=False, gives="", given=None, in_place=False):
    rows, heads, size = shape
    js, tall = heads // EIGHT, rows * EIGHT
    arrays, blocks_of = [], []
    for block in kvs:
        block = block if isinstance(block, tuple) else (block,)
        blocks_of.append((len(arrays), len(arrays) + len(block) - 1))
        arrays += block
    inputs = [*prepared, *state, *arrays]
    specs = [VMEM] * len(inputs)
    outs = [jax.ShapeDtypeStruct((js, tall, LANES), jnp.float32)] * (3 if keeps else 0)
    out_specs = [VMEM] * len(outs)
    aliases = {2: 0, 3: 1, 4: 2} if in_place else {}
    if gives == "given":
        aliases[len(inputs)] = len(outs)
        inputs.append(given)
        specs.append(ANY)
    if gives:
        outs.append(jax.ShapeDtypeStruct(shape, jnp.bfloat16))
        out_specs.append(ANY)
    scale = LOG2E * size ** (-0.5)
    return pl.pallas_call(
        functools.partial(attend_kernel, cases, scale, bool(state), keeps, gives, blocks_of),
        out_shape=tuple(outs),
        in_specs=specs,
        out_specs=tuple(out_specs),
        input_output_aliases=aliases,
        scratch_shapes=[pltpu.VMEM(shape, jnp.bfloat16), pltpu.SemaphoreType.DMA((rows // SMALL, js // 2))] if gives else [],
        compiler_params=pltpu.CompilerParams(vmem_limit_bytes=24 * MIB),
        cost_estimate=pl.CostEstimate(flops=1024, bytes_accessed=1024, transcendentals=0),
        name=name,
    )(*inputs)


def on_device(axes, dp, ctx, queries, keys, values, doc_blocks):
    assert queries.shape[0] == queries.shape[2]
    *prepared, own, longer, longest = prepare(doc_blocks, queries, keys, values, (0, 8, 16))
    call = functools.partial(attend, shape=queries.shape, prepared=prepared)
    count, farthest = dp * ctx, dp // 2 - 1
    def moved(array, target_of):
        def at(block):
            return block % dp * ctx + block // dp if axes[0] == "dp" else block

        route = [(i, target_of(i)) for i in range(count)]
        return lax.ppermute(array, axes, [(at(i), at(to)) for i, to in route if to is not None and to < count])

    if farthest == 3:
        crossed = [moved(part, lambda i: i + 1 if i % 2 else i + 3) for part in (keys, values)]
        state = call("own_sums", kvs=[own], cases=[([(None, 1, None)], [0], False)], keeps=True)
        beside = moved(longest, lambda i: None if i % 2 else i + 1)
        longer, state = lax.optimization_barrier((longer, state))
        behind = moved(longer, lambda i: i + 3 if i % 2 else None)
        (out,) = call("own_output", kvs=[own], cases=[([(None, 0, 1)], [0], True)], gives="fresh")
        crossed = pack(*crossed)
        crossed, state, out = lax.optimization_barrier((crossed, state, out))
        swapped = moved(crossed, lambda i: i ^ 1)
        cases = [
            ([(0, 1, 2)], [0], True),
            ([(0, 2, None)], [0], False),
            ([(1, 1, 2)], [1], True),
            ([(1, 2, None)], [1], False),
        ]
        *state, out = call(
            "nearest", kvs=[crossed, beside], cases=cases, state=state, keeps=True, gives="given", given=out
        )
        cases = [
            ([(None, 2, 3)], [1], True),
            ([(0, 3, None)], [1], False),
            ([(1, 3, None)], [1, 0], True),
        ]
        *state, out = call(
            "swapped_blocks", kvs=[crossed, swapped], cases=cases, state=state, keeps=True, gives="given", given=out
        )
        cases = [([(0, 3, None)], [0], True)]
        (out,) = call("farthest", kvs=[behind], cases=cases, state=state, gives="given", given=out)
        return out
    state = call("own_blocks", kvs=[own], cases=[([(None, 0, None)], [0], False)], keeps=True)
    shifted = [moved(own, lambda i, m=m: i + 2 * m) for m in range(1, (farthest - 1) // 2 + 1)]
    alone = moved(longer, lambda i: i + farthest if i % 2 else i + 1)
    shifted, state = lax.optimization_barrier((shifted, state))
    for m, block in enumerate(shifted, 1):
        other = moved(block, lambda i: i ^ 1)
        cases = [
            ([(0, 2 * m - 1, 2 * m)], [1], False),
            ([(0, 2 * m, None), (1, 2 * m + 1, None)], [0, 1], False),
            ([(1, 2 * m, 2 * m + 1)], [0], False),
        ]
        state = call("more_blocks", kvs=[block, other], cases=cases, state=state, keeps=True, in_place=True)
    cases = [
        ([(0, farthest, None), (1, 1, None)], [0], True),
        ([(0, 0, farthest), (1, 0, 1)], [], True),
    ]
    (out,) = call("farthest", kvs=[alone], cases=cases, state=state, gives="fresh")
    return out


def solution(mesh):
    dp, ctx = mesh.shape["dp"], mesh.shape["ctx"]
    placed = P(("ctx", "dp"), None, None)
    return jax.shard_map(
        functools.partial(on_device, tuple(mesh.axis_names), dp, ctx),
        mesh=mesh,
        in_specs=(placed, placed, placed, P()),
        out_specs=placed,
        check_vma=False,
    )
```

```python
import functools

import jax
import jax.numpy as jnp
from jax import lax
from jax.experimental import pallas as pl
from jax.experimental.pallas import tpu as pltpu
from jax.sharding import PartitionSpec as P

LOG2E = 1.4426950408889634
MIB = 1 << 20
VMEM = pl.BlockSpec(memory_space=pltpu.VMEM)
SMEM = pl.BlockSpec(memory_space=pltpu.SMEM)
ANY = pl.BlockSpec(memory_space=pl.ANY)
HBM = pl.BlockSpec(memory_space=pltpu.HBM)
LANES = 128
GROUP = 4
EIGHT = 2 * GROUP
LARGE, SMALL = 64, 32


def lay_out(refs, wide, write):
    for n, ref in enumerate(refs):
        rows, heads, size = ref.shape
        wide[n, : rows * heads] = ref[...].astype(jnp.float32).reshape(rows * heads, size)
        for g in range(heads):
            part = wide[n, pl.ds(g, rows, stride=heads), :].astype(jnp.bfloat16)
            write(n, g, part.T if n == 0 else part)


def put(ref, heads, n, g, part):
    rows, size = part.shape
    if ref.shape[1] == size:
        ref[(n * heads + g) * rows : (n * heads + g + 1) * rows, :] = part
    else:
        ref[n * rows : (n + 1) * rows, g * size : (g + 1) * size] = part


def pack_kernel(k_ref, v_ref, out_ref, wide):
    lay_out((k_ref, v_ref), wide, functools.partial(put, out_ref, k_ref.shape[1]))


def pack(keys, values):
    rows, heads, size = keys.shape
    return pl.pallas_call(
        pack_kernel,
        out_shape=jax.ShapeDtypeStruct((2 * rows, heads * size), jnp.bfloat16),
        in_specs=[VMEM, VMEM],
        out_specs=VMEM,
        scratch_shapes=[pltpu.VMEM((2, (rows + 1) * heads, size), jnp.float32)],
        compiler_params=pltpu.CompilerParams(vmem_limit_bytes=8 * MIB),
        cost_estimate=pl.CostEstimate(flops=1024, bytes_accessed=1024, transcendentals=0),
        name="pack_kv",
    )(keys, values)


def blocks_before(doc_ref, block):
    def step(j, carry):
        end, start = carry
        end = end + doc_ref[j]
        return end, jnp.where(end <= block, end, start)

    _, start = lax.fori_loop(0, doc_ref.shape[0], step, (jnp.int32(0), jnp.int32(0)))
    return block - start


def low_rows(rows, lanes):
    return lax.broadcasted_iota(jnp.int32, (rows, lanes), 0) % EIGHT < GROUP


def stacked(ref, n, j, rows):
    if ref.shape[1] == rows:
        first = n * (ref.shape[0] // rows // 2) + 2 * j
        return ref[first * rows : (first + 2) * rows, :]
    top = n * rows if ref.shape[0] > rows else 0
    lanes = [slice(g * rows, (g + 1) * rows) for g in (2 * j, 2 * j + 1)]
    return jnp.concatenate([ref[top : top + rows, lane] for lane in lanes], axis=0)


def keys_of(blocks, j, rows):
    return jnp.concatenate([stacked(ref, 0, j, rows) for ref, _ in blocks], axis=1)


def values_of(blocks, j, rows):
    lanes = slice(2 * j * rows, 2 * (j + 1) * rows)
    tops = [rows if ref.shape[0] > rows else 0 for _, ref in blocks]
    return jnp.concatenate([ref[top : top + rows, lanes] for top, (_, ref) in zip(tops, blocks)], axis=0)


def dot(a, b):
    return jnp.dot(a, b, preferred_element_type=jnp.float32)


def prepare_kernel(doc_ref, q_ref, k_ref, v_ref, lhs_ref, before_ref, *refs):
    *out_refs, lengths, near_q, near_k, near_v, wide, sems = refs
    rows, heads, size = near_q.shape
    tall = SMALL * EIGHT
    low = low_rows(tall, size)
    spans = [pl.ds(t * SMALL, SMALL) for t in range(rows // SMALL)]
    pairs = [(k_ref, near_k), (v_ref, near_v), (doc_ref, lengths)]
    pairs += [(q_ref.at[span], near_q.at[span]) for span in spans]
    copies = [pltpu.make_async_copy(*pair, sems.at[n]) for n, pair in enumerate(pairs)]
    for copy in copies:
        copy.start()
    for copy in copies[:3]:
        copy.wait()

    def write(*where):
        for ref in out_refs:
            put(ref, near_k.shape[1], *where)

    lay_out((near_k, near_v), wide, write)
    block = lax.axis_index("ctx") * lax.axis_size("dp") + lax.axis_index("dp")
    before_ref[...] = jnp.full(before_ref.shape, blocks_before(lengths, block), jnp.int32)
    for t, span in enumerate(spans):
        copies[3 + t].wait()
        for j in range(heads // EIGHT):
            if j % 2 == 0:
                q16 = near_q[span, j * EIGHT : (j + 2) * EIGHT, :].astype(jnp.float32)
            q8 = q16[:, j % 2 * EIGHT : (j % 2 + 1) * EIGHT, :].reshape(tall, size)
            lhs = jnp.concatenate([jnp.where(low, q8, 0.0), jnp.where(low, 0.0, q8)], axis=1)
            lhs_ref[j, t * tall : (t + 1) * tall, :] = lhs.astype(jnp.bfloat16)


def prepare(doc_blocks, queries, keys, values, shapes):
    rows, heads, size = queries.shape
    kv_heads = keys.shape[1]
    arrays = [pltpu.with_memory_space_constraint(x, pltpu.HBM) for x in (doc_blocks, queries, keys, values)]
    return pl.pallas_call(
        prepare_kernel,
        out_shape=(
            jax.ShapeDtypeStruct((heads // EIGHT, rows * EIGHT, 2 * size), jnp.bfloat16),
            jax.ShapeDtypeStruct((EIGHT, LANES), jnp.int32),
            *(jax.ShapeDtypeStruct(shape, jnp.bfloat16) for shape in shapes),
        ),
        in_specs=[HBM] * 4,
        out_specs=(VMEM,) * (2 + len(shapes)),
        scratch_shapes=[
            pltpu.SMEM(doc_blocks.shape, jnp.int32),
            pltpu.VMEM(queries.shape, jnp.bfloat16),
            pltpu.VMEM(keys.shape, jnp.bfloat16),
            pltpu.VMEM(values.shape, jnp.bfloat16),
            pltpu.VMEM((2, (rows + 1) * kv_heads, size), jnp.float32),
            pltpu.SemaphoreType.DMA((rows // SMALL + 3,)),
        ],
        compiler_params=pltpu.CompilerParams(vmem_limit_bytes=16 * MIB),
        cost_estimate=pl.CostEstimate(flops=1024, bytes_accessed=1024, transcendentals=0),
        name="prepare",
    )(*arrays)


def attend_kernel(cases, scale, merges, keeps, gives, blocks_of, *refs):
    refs = list(refs)
    lhs_ref, before_ref = refs[:2]
    del refs[:2]
    if merges:
        state_ref = refs[:3]
        del refs[:3]
    count = max(at for block in blocks_of for at in block) + 1
    given = [(refs[a], refs[b]) for a, b in blocks_of]
    del refs[:count]
    if gives == "given":
        del refs[0]
    if keeps:
        state_out = refs[:3]
        del refs[:3]
    if gives:
        out_ref, held, sems = refs
    js, size = lhs_ref.shape[0], lhs_ref.shape[2] // 2
    rows = lhs_ref.shape[1] // EIGHT
    place = lax.axis_index("dp")
    before = jnp.max(before_ref[...])

    def out_copy(t, pair, tile):
        part = pl.ds(t * tile, tile), pl.ds(pair * 2 * EIGHT, 2 * EIGHT)
        return pltpu.make_async_copy(held.at[part], out_ref.at[part], sems.at[t, pair])

    def add(blocks, last):
        tile = SMALL if len(blocks) < 2 else LARGE
        tall = tile * EIGHT
        low = low_rows(tall, size)
        if not merges:
            token = lax.broadcasted_iota(jnp.int32, (tall, rows), 0) // EIGHT
            spot = lax.broadcasted_iota(jnp.int32, (tall, rows), 1)
        for t in range(rows // tile):
            tokens, here, outs = pl.ds(t * tile, tile), pl.ds(t * tall, tall), []
            for j in range(js):
                if merges:
                    old, total, mixed = (ref[j, here, :] for ref in state_ref)
                if blocks:
                    s = dot(lhs_ref[j, here, :], keys_of(blocks, j, rows))
                    s = [s[:, n * rows : (n + 1) * rows] for n in range(len(blocks))]
                    if not merges:
                        s[0] = jnp.where(spot <= token + t * tile, s[0], -jnp.inf)
                    top = jnp.max(functools.reduce(jnp.maximum, s), axis=1, keepdims=True)
                    if merges:
                        top = jnp.maximum(old, top)
                        keep = jnp.exp2((old - top) * scale)
                    w = [jnp.exp2((part - top) * scale) for part in s]
                    if len(blocks) == 1:
                        halves = [jnp.where(low, w[0], 0.0), jnp.where(low, 0.0, w[0])]
                        found = dot(jnp.concatenate(halves, axis=1).astype(jnp.bfloat16), stacked(blocks[0][1], 1, j, rows))
                    else:
                        found = dot(jnp.concatenate(w, axis=1).astype(jnp.bfloat16), values_of(blocks, j, rows))
                        found = jnp.where(low, found[:, :size], found[:, size:])
                    fresh = functools.reduce(jnp.add, w)
                    mixed = found + keep * mixed if merges else found
                    total = fresh + keep * total if merges else fresh
                if last:
                    total = jnp.sum(total, axis=1, keepdims=True)
                    outs.append((mixed * pl.reciprocal(total, approx=True)).reshape(tile, EIGHT, size))
                    if j % 2:
                        held[tokens, (j - 1) * EIGHT : (j + 1) * EIGHT, :] = jnp.concatenate(
                            outs[-2:], axis=1
                        ).astype(jnp.bfloat16)
                        out_copy(t, j // 2, tile).start()
                else:
                    state_out[0][j, here, :] = jnp.broadcast_to(top, (tall, LANES))
                    state_out[1][j, here, :] = total
                    state_out[2][j, here, :] = mixed
        if last:
            for t in range(rows // tile):
                for pair in range(js // 2):
                    out_copy(t, pair, tile).wait()

    for wheres, chosen, last in cases:
        fits = False
        for parity, least, end in wheres:
            fit = before >= least
            if end is not None:
                fit = jnp.logical_and(fit, before < end)
            if parity is not None:
                fit = jnp.logical_and(fit, place % 2 == parity)
            fits = fit if fits is False else jnp.logical_or(fits, fit)
        pl.when(fits)(functools.partial(add, [given[at] for at in chosen], last))


def attend(name, shape, prepared, kvs, cases, state=(), keeps=False, gives="", given=None, in_place=False):
    rows, heads, size = shape
    js, tall = heads // EIGHT, rows * EIGHT
    arrays, blocks_of = [], []
    for block in kvs:
        block = block if isinstance(block, tuple) else (block,)
        blocks_of.append((len(arrays), len(arrays) + len(block) - 1))
        arrays += block
    inputs = [*prepared, *state, *arrays]
    specs = [VMEM] * len(inputs)
    outs = [jax.ShapeDtypeStruct((js, tall, LANES), jnp.float32)] * (3 if keeps else 0)
    out_specs = [VMEM] * len(outs)
    aliases = {2: 0, 3: 1, 4: 2} if in_place else {}
    if gives == "given":
        aliases[len(inputs)] = len(outs)
        inputs.append(given)
        specs.append(ANY)
    if gives:
        outs.append(jax.ShapeDtypeStruct(shape, jnp.bfloat16))
        out_specs.append(ANY)
    scale = LOG2E * size ** (-0.5)
    return pl.pallas_call(
        functools.partial(attend_kernel, cases, scale, bool(state), keeps, gives, blocks_of),
        out_shape=tuple(outs),
        in_specs=specs,
        out_specs=tuple(out_specs),
        input_output_aliases=aliases,
        scratch_shapes=[pltpu.VMEM(shape, jnp.bfloat16), pltpu.SemaphoreType.DMA((rows // SMALL, js // 2))] if gives else [],
        compiler_params=pltpu.CompilerParams(vmem_limit_bytes=24 * MIB),
        cost_estimate=pl.CostEstimate(flops=1024, bytes_accessed=1024, transcendentals=0),
        name=name,
    )(*inputs)


def on_device(axes, dp, ctx, queries, keys, values, doc_blocks):
    assert queries.shape[0] == queries.shape[2]
    rows, wide = 2 * keys.shape[0], keys.shape[1] * keys.shape[2]
    tall = rows * keys.shape[1] + 8, keys.shape[2]
    *prepared, own, longer, longest = prepare(doc_blocks, queries, keys, values, ((rows, wide), tall, (rows + 16, wide)))
    call = functools.partial(attend, shape=queries.shape, prepared=prepared)
    count, farthest = dp * ctx, dp // 2 - 1
    def moved(array, target_of):
        def at(block):
            return block % dp * ctx + block // dp if axes[0] == "dp" else block

        route = [(i, target_of(i)) for i in range(count)]
        return lax.ppermute(array, axes, [(at(i), at(to)) for i, to in route if to is not None and to < count])

    if farthest == 3:
        crossed = [moved(part, lambda i: i + 1 if i % 2 else i + 3) for part in (keys, values)]
        state = call("own_sums", kvs=[own], cases=[([(None, 1, None)], [0], False)], keeps=True)
        beside = moved(longest, lambda i: None if i % 2 else i + 1)
        longer, state = lax.optimization_barrier((longer, state))
        behind = moved(longer, lambda i: i + 3 if i % 2 else None)
        (out,) = call("own_output", kvs=[own], cases=[([(None, 0, 1)], [0], True)], gives="fresh")
        crossed = pack(*crossed)
        crossed, state, out = lax.optimization_barrier((crossed, state, out))
        swapped = moved(crossed, lambda i: i ^ 1)
        cases = [
            ([(0, 1, 2)], [0], True),
            ([(0, 2, None)], [0], False),
            ([(1, 1, 2)], [1], True),
            ([(1, 2, None)], [1], False),
        ]
        *state, out = call(
            "nearest", kvs=[crossed, beside], cases=cases, state=state, keeps=True, gives="given", given=out
        )
        cases = [
            ([(None, 2, 3)], [1], True),
            ([(0, 3, None)], [1], False),
            ([(1, 3, None)], [1, 0], True),
        ]
        *state, out = call(
            "swapped_blocks", kvs=[crossed, swapped], cases=cases, state=state, keeps=True, gives="given", given=out
        )
        cases = [([(0, 3, None)], [0], True)]
        (out,) = call("farthest", kvs=[behind], cases=cases, state=state, gives="given", given=out)
        return out
    state = call("own_blocks", kvs=[own], cases=[([(None, 0, None)], [0], False)], keeps=True)
    shifted = [moved(own, lambda i, m=m: i + 2 * m) for m in range(1, (farthest - 1) // 2 + 1)]
    alone = moved(longer, lambda i: i + farthest if i % 2 else i + 1)
    shifted, state = lax.optimization_barrier((shifted, state))
    for m, block in enumerate(shifted, 1):
        other = moved(block, lambda i: i ^ 1)
        cases = [
            ([(0, 2 * m - 1, 2 * m)], [1], False),
            ([(0, 2 * m, None), (1, 2 * m + 1, None)], [0, 1], False),
            ([(1, 2 * m, 2 * m + 1)], [0], False),
        ]
        state = call("more_blocks", kvs=[block, other], cases=cases, state=state, keeps=True, in_place=True)
    cases = [
        ([(0, farthest, None), (1, 1, None)], [0], True),
        ([(0, 0, farthest), (1, 0, 1)], [], True),
    ]
    (out,) = call("farthest", kvs=[alone], cases=cases, state=state, gives="fresh")
    return out


def solution(mesh):
    dp, ctx = mesh.shape["dp"], mesh.shape["ctx"]
    placed = P(("ctx", "dp"), None, None)
    return jax.shard_map(
        functools.partial(on_device, tuple(mesh.axis_names), dp, ctx),
        mesh=mesh,
        in_specs=(placed, placed, placed, P()),
        out_specs=placed,
        check_vma=False,
    )
```

```python
import functools

import jax
import jax.numpy as jnp
from jax import lax
from jax.experimental import pallas as pl
from jax.experimental.pallas import tpu as pltpu
from jax.sharding import PartitionSpec as P

LOG2E = 1.4426950408889634
MIB = 1 << 20
VMEM = pl.BlockSpec(memory_space=pltpu.VMEM)
SMEM = pl.BlockSpec(memory_space=pltpu.SMEM)
ANY = pl.BlockSpec(memory_space=pl.ANY)
HBM = pl.BlockSpec(memory_space=pltpu.HBM)
LANES = 128
GROUP = 4
EIGHT = 2 * GROUP
LARGE, SMALL = 64, 32


def lay_out(refs, wide, write):
    for n, ref in enumerate(refs):
        rows, heads, size = ref.shape
        wide[n, : rows * heads] = ref[...].astype(jnp.float32).reshape(rows * heads, size)
        for g in range(heads):
            part = wide[n, pl.ds(g, rows, stride=heads), :].astype(jnp.bfloat16)
            write(n, g, part.T if n == 0 else part)


def put(ref, heads, n, g, part):
    rows, size = part.shape
    if ref.shape[1] == size:
        ref[(n * heads + g) * rows : (n * heads + g + 1) * rows, :] = part
    else:
        ref[n * rows : (n + 1) * rows, g * size : (g + 1) * size] = part


def pack_kernel(k_ref, v_ref, out_ref, wide):
    lay_out((k_ref, v_ref), wide, functools.partial(put, out_ref, k_ref.shape[1]))


def pack(keys, values):
    rows, heads, size = keys.shape
    return pl.pallas_call(
        pack_kernel,
        out_shape=jax.ShapeDtypeStruct((2 * rows, heads * size), jnp.bfloat16),
        in_specs=[VMEM, VMEM],
        out_specs=VMEM,
        scratch_shapes=[pltpu.VMEM((2, (rows + 1) * heads, size), jnp.float32)],
        compiler_params=pltpu.CompilerParams(vmem_limit_bytes=8 * MIB),
        cost_estimate=pl.CostEstimate(flops=1024, bytes_accessed=1024, transcendentals=0),
        name="pack_kv",
    )(keys, values)


def blocks_before(doc_ref, block):
    def step(j, carry):
        end, start = carry
        end = end + doc_ref[j]
        return end, jnp.where(end <= block, end, start)

    _, start = lax.fori_loop(0, doc_ref.shape[0], step, (jnp.int32(0), jnp.int32(0)))
    return block - start


def low_rows(rows, lanes):
    return lax.broadcasted_iota(jnp.int32, (rows, lanes), 0) % EIGHT < GROUP


def heads_of(ref, n, j, rows):
    if ref.shape[1] == rows:
        first = n * (ref.shape[0] // rows // 2) + 2 * j
        return [ref[g * rows : (g + 1) * rows, :] for g in (first, first + 1)]
    return [ref[n * rows : (n + 1) * rows, g * rows : (g + 1) * rows] for g in (2 * j, 2 * j + 1)]


def keys_of(blocks, j, rows):
    return jnp.concatenate([jnp.concatenate(heads_of(ref, 0, j, rows), axis=0) for ref in blocks], axis=1)


def values_of(blocks, j, rows):
    return jnp.concatenate([jnp.concatenate(heads_of(ref, 1, j, rows), axis=1) for ref in blocks], axis=0)


def dot(a, b):
    return jnp.dot(a, b, preferred_element_type=jnp.float32)


def prepare_kernel(doc_ref, q_ref, k_ref, v_ref, lhs_ref, before_ref, *refs):
    *out_refs, lengths, near_q, near_k, near_v, wide, sems = refs
    rows, heads, size = near_q.shape
    tall = SMALL * EIGHT
    low = low_rows(tall, size)
    spans = [pl.ds(t * SMALL, SMALL) for t in range(rows // SMALL)]
    pairs = [(k_ref, near_k), (v_ref, near_v), (doc_ref, lengths)]
    pairs += [(q_ref.at[span], near_q.at[span]) for span in spans]
    copies = [pltpu.make_async_copy(*pair, sems.at[n]) for n, pair in enumerate(pairs)]
    for copy in copies:
        copy.start()
    for copy in copies[:3]:
        copy.wait()

    def write(*where):
        for ref in out_refs:
            put(ref, near_k.shape[1], *where)

    lay_out((near_k, near_v), wide, write)
    block = lax.axis_index("ctx") * lax.axis_size("dp") + lax.axis_index("dp")
    before_ref[...] = jnp.full(before_ref.shape, blocks_before(lengths, block), jnp.int32)
    for t, span in enumerate(spans):
        copies[3 + t].wait()
        for j in range(heads // EIGHT):
            if j % 2 == 0:
                q16 = near_q[span, j * EIGHT : (j + 2) * EIGHT, :].astype(jnp.float32)
            q8 = q16[:, j % 2 * EIGHT : (j % 2 + 1) * EIGHT, :].reshape(tall, size)
            lhs = jnp.concatenate([jnp.where(low, q8, 0.0), jnp.where(low, 0.0, q8)], axis=1)
            lhs_ref[j, t * tall : (t + 1) * tall, :] = lhs.astype(jnp.bfloat16)


def prepare(doc_blocks, queries, keys, values, shapes):
    rows, heads, size = queries.shape
    kv_heads = keys.shape[1]
    arrays = [pltpu.with_memory_space_constraint(x, pltpu.HBM) for x in (doc_blocks, queries, keys, values)]
    return pl.pallas_call(
        prepare_kernel,
        out_shape=(
            jax.ShapeDtypeStruct((heads // EIGHT, rows * EIGHT, 2 * size), jnp.bfloat16),
            jax.ShapeDtypeStruct((EIGHT, LANES), jnp.int32),
            *(jax.ShapeDtypeStruct(shape, jnp.bfloat16) for shape in shapes),
        ),
        in_specs=[HBM] * 4,
        out_specs=(VMEM,) * (2 + len(shapes)),
        scratch_shapes=[
            pltpu.SMEM(doc_blocks.shape, jnp.int32),
            pltpu.VMEM(queries.shape, jnp.bfloat16),
            pltpu.VMEM(keys.shape, jnp.bfloat16),
            pltpu.VMEM(values.shape, jnp.bfloat16),
            pltpu.VMEM((2, (rows + 1) * kv_heads, size), jnp.float32),
            pltpu.SemaphoreType.DMA((rows // SMALL + 3,)),
        ],
        compiler_params=pltpu.CompilerParams(vmem_limit_bytes=16 * MIB),
        cost_estimate=pl.CostEstimate(flops=1024, bytes_accessed=1024, transcendentals=0),
        name="prepare",
    )(*arrays)


def attend_kernel(cases, scale, merges, keeps, gives, count, *refs):
    refs = list(refs)
    lhs_ref, before_ref = refs[:2]
    del refs[:2]
    if merges:
        state_ref = refs[:3]
        del refs[:3]
    given = refs[:count]
    del refs[:count]
    if gives == "given":
        del refs[0]
    if keeps:
        state_out = refs[:3]
        del refs[:3]
    if gives:
        out_ref, held, sems = refs
    js, size = lhs_ref.shape[0], lhs_ref.shape[2] // 2
    rows = lhs_ref.shape[1] // EIGHT
    place = lax.axis_index("dp")
    before = jnp.max(before_ref[...])

    def out_copy(t, pair, tile):
        part = pl.ds(t * tile, tile), pl.ds(pair * 2 * EIGHT, 2 * EIGHT)
        return pltpu.make_async_copy(held.at[part], out_ref.at[part], sems.at[t, pair])

    def add(blocks, last):
        tile = SMALL if len(blocks) < 2 else LARGE
        tall = tile * EIGHT
        low = low_rows(tall, size)
        if not merges:
            token = lax.broadcasted_iota(jnp.int32, (tall, rows), 0) // EIGHT
            spot = lax.broadcasted_iota(jnp.int32, (tall, rows), 1)
        for t in range(rows // tile):
            tokens, here, outs = pl.ds(t * tile, tile), pl.ds(t * tall, tall), []
            for j in range(js):
                if merges:
                    old, total, mixed = (ref[j, here, :] for ref in state_ref)
                if blocks:
                    s = dot(lhs_ref[j, here, :], keys_of(blocks, j, rows))
                    s = [s[:, n * rows : (n + 1) * rows] for n in range(len(blocks))]
                    if not merges:
                        s[0] = jnp.where(spot <= token + t * tile, s[0], -jnp.inf)
                    top = jnp.max(functools.reduce(jnp.maximum, s), axis=1, keepdims=True)
                    if merges:
                        top = jnp.maximum(old, top)
                        keep = jnp.exp2((old - top) * scale)
                    w = [jnp.exp2((part - top) * scale) for part in s]
                    found = dot(jnp.concatenate(w, axis=1).astype(jnp.bfloat16), values_of(blocks, j, rows))
                    found = jnp.where(low, found[:, :size], found[:, size:])
                    fresh = functools.reduce(jnp.add, w)
                    mixed = found + keep * mixed if merges else found
                    total = fresh + keep * total if merges else fresh
                if last:
                    total = jnp.sum(total, axis=1, keepdims=True)
                    outs.append((mixed * pl.reciprocal(total, approx=True)).reshape(tile, EIGHT, size))
                    if j % 2:
                        held[tokens, (j - 1) * EIGHT : (j + 1) * EIGHT, :] = jnp.concatenate(
                            outs[-2:], axis=1
                        ).astype(jnp.bfloat16)
                        out_copy(t, j // 2, tile).start()
                else:
                    state_out[0][j, here, :] = jnp.broadcast_to(top, (tall, LANES))
                    state_out[1][j, here, :] = total
                    state_out[2][j, here, :] = mixed
        if last:
            for t in range(rows // tile):
                for pair in range(js // 2):
                    out_copy(t, pair, tile).wait()

    for wheres, chosen, last in cases:
        fits = False
        for parity, least, end in wheres:
            fit = before >= least
            if end is not None:
                fit = jnp.logical_and(fit, before < end)
            if parity is not None:
                fit = jnp.logical_and(fit, place % 2 == parity)
            fits = fit if fits is False else jnp.logical_or(fits, fit)
        pl.when(fits)(functools.partial(add, [given[at] for at in chosen], last))


def attend(name, shape, prepared, kvs, cases, state=(), keeps=False, gives="", given=None, in_place=False):
    rows, heads, size = shape
    js, tall = heads // EIGHT, rows * EIGHT
    inputs = [*prepared, *state, *kvs]
    specs = [VMEM] * len(inputs)
    outs = [jax.ShapeDtypeStruct((js, tall, LANES), jnp.float32)] * (3 if keeps else 0)
    out_specs = [VMEM] * len(outs)
    aliases = {2: 0, 3: 1, 4: 2} if in_place else {}
    if gives == "given":
        aliases[len(inputs)] = len(outs)
        inputs.append(given)
        specs.append(ANY)
    if gives:
        outs.append(jax.ShapeDtypeStruct(shape, jnp.bfloat16))
        out_specs.append(ANY)
    scale = LOG2E * size ** (-0.5)
    return pl.pallas_call(
        functools.partial(attend_kernel, cases, scale, bool(state), keeps, gives, len(kvs)),
        out_shape=tuple(outs),
        in_specs=specs,
        out_specs=tuple(out_specs),
        input_output_aliases=aliases,
        scratch_shapes=[pltpu.VMEM(shape, jnp.bfloat16), pltpu.SemaphoreType.DMA((rows // SMALL, js // 2))] if gives else [],
        compiler_params=pltpu.CompilerParams(vmem_limit_bytes=24 * MIB),
        cost_estimate=pl.CostEstimate(flops=1024, bytes_accessed=1024, transcendentals=0),
        name=name,
    )(*inputs)


def on_device(axes, dp, ctx, queries, keys, values, doc_blocks):
    assert queries.shape[0] == queries.shape[2]
    rows, wide = 2 * keys.shape[0], keys.shape[1] * keys.shape[2]
    tall = rows * keys.shape[1] + 8, keys.shape[2]
    *prepared, own, longer, longest = prepare(doc_blocks, queries, keys, values, ((rows, wide), tall, (rows + 16, wide)))
    call = functools.partial(attend, shape=queries.shape, prepared=prepared)
    count, farthest = dp * ctx, dp // 2 - 1
    def moved(array, target_of):
        def at(block):
            return block % dp * ctx + block // dp if axes[0] == "dp" else block

        route = [(i, target_of(i)) for i in range(count)]
        return lax.ppermute(array, axes, [(at(i), at(to)) for i, to in route if to is not None and to < count])

    if farthest == 3:
        crossed = [moved(part, lambda i: i + 1 if i % 2 else i + 3) for part in (keys, values)]
        state = call("own_sums", kvs=[own], cases=[([(None, 1, None)], [0], False)], keeps=True)
        beside = moved(longest, lambda i: None if i % 2 else i + 1)
        longer, state = lax.optimization_barrier((longer, state))
        behind = moved(longer, lambda i: i + 3 if i % 2 else None)
        (out,) = call("own_output", kvs=[own], cases=[([(None, 0, 1)], [0], True)], gives="fresh")
        crossed = pack(*crossed)
        crossed, state, out = lax.optimization_barrier((crossed, state, out))
        swapped = moved(crossed, lambda i: i ^ 1)
        cases = [
            ([(0, 1, 2)], [0], True),
            ([(0, 2, None)], [0], False),
            ([(1, 1, 2)], [1], True),
            ([(1, 2, None)], [1], False),
        ]
        *state, out = call(
            "nearest", kvs=[crossed, beside], cases=cases, state=state, keeps=True, gives="given", given=out
        )
        cases = [
            ([(None, 2, 3)], [1], True),
            ([(0, 3, None)], [1], False),
            ([(1, 3, None)], [1, 0], True),
        ]
        *state, out = call(
            "swapped_blocks", kvs=[crossed, swapped], cases=cases, state=state, keeps=True, gives="given", given=out
        )
        cases = [([(0, 3, None)], [0], True)]
        (out,) = call("farthest", kvs=[behind], cases=cases, state=state, gives="given", given=out)
        return out
    state = call("own_blocks", kvs=[own], cases=[([(None, 0, None)], [0], False)], keeps=True)
    shifted = [moved(own, lambda i, m=m: i + 2 * m) for m in range(1, (farthest - 1) // 2 + 1)]
    alone = moved(longer, lambda i: i + farthest if i % 2 else i + 1)
    shifted, state = lax.optimization_barrier((shifted, state))
    for m, block in enumerate(shifted, 1):
        other = moved(block, lambda i: i ^ 1)
        cases = [
            ([(0, 2 * m - 1, 2 * m)], [1], False),
            ([(0, 2 * m, None), (1, 2 * m + 1, None)], [0, 1], False),
            ([(1, 2 * m, 2 * m + 1)], [0], False),
        ]
        state = call("more_blocks", kvs=[block, other], cases=cases, state=state, keeps=True, in_place=True)
    cases = [
        ([(0, farthest, None), (1, 1, None)], [0], True),
        ([(0, 0, farthest), (1, 0, 1)], [], True),
    ]
    (out,) = call("farthest", kvs=[alone], cases=cases, state=state, gives="fresh")
    return out


def solution(mesh):
    dp, ctx = mesh.shape["dp"], mesh.shape["ctx"]
    placed = P(("ctx", "dp"), None, None)
    return jax.shard_map(
        functools.partial(on_device, tuple(mesh.axis_names), dp, ctx),
        mesh=mesh,
        in_specs=(placed, placed, placed, P()),
        out_specs=placed,
        check_vma=False,
    )
```
